32 devices in a mesh: groups: 2 (over y), row: 4 (over x, core), col: 4 (over z).
Axes of the slice: x: 2, y: 2, z: 4, core: 2. Of those that a mesh axis runs over, the one named last changes fastest.
Arguments:
- features: bfloat16 [8, 4, 256, 256], P(('groups', 'col'), 'row'), parts along dimension 0, may hold values from -6 to 6
- weight: bfloat16 [256, 256], replicated, may hold values from -0.375 to 0.375
- bias: float32 [256], replicated, may hold values from -3 to 3
- tile_rows: int32 [8, 4, 128], P(('groups', 'row'), 'col'), parts along dimension 0, may hold values from 0 to 7
- tile_cols: int32 [8, 4, 128], P(('groups', 'row'), 'col'), parts along dimension 0, may hold values from 0 to 7
- tile_vals: bfloat16 [8, 4, 128, 128, 128], P(('groups', 'row'), 'col'), parts along dimension 0, may hold values from -0.0625 to 0.0625
- tile_count: int32 [8, 4], P(('groups', 'row'), 'col'), parts along dimension 0, may hold values from 32 to 128, as said below
- cotangent: bfloat16 [8, 4, 256, 256], P(('groups', 'row'), 'col'), parts along dimension 0, may hold values from -6 to 6
Outputs:
- hidden: bfloat16 [8, 4, 256, 256], P(('groups', 'row'), 'col'), parts along dimension 0
- grad_features: bfloat16 [8, 4, 256, 256], P(('groups', 'col'), 'row'), parts along dimension 0
- grad_weight: float32 [512, 256], P('groups'), parts along dimension 0
- grad_bias: float32 [512], P('groups'), parts along dimension 0
The draws below stay inside these ranges and needn't reach their ends.
There are 2 independent parts, one for each index of `groups`. The reference program is written for one: setup_inputs(seed, part) draws one part's arguments, and reference() takes and returns one part's arrays. A program takes and returns all parts, laid end to end along the dimension named above; an argument that names none is the same for every part. Nothing has to cross between parts.
Inputs may be any that keep to these rules, and one draw needn't show every extreme that they name: `tile_count`: some grid block has all 128 slots live.
All inputs are finite; a program needn't handle non-finite values.
Results may differ from the reference program's by a relative error of at most 0.024.
Values may be sent and summed in bfloat16 or wider, within the bound.
No kernel may reach another device: no remote copies, remote signals or barrier semaphores. Data moves between devices by JAX's collectives and lax.ppermute only.
A program may use at most 64 MiB of HBM per device.

```python
import math
import jax
import jax.numpy as jnp
import numpy as np
from jax import lax

FEAT = 256
TILE = 128
ROWS_DEV = 256
TILES = 128
TILE_ROWS = 8
NODES = 4096
N_ROW = 4
N_COL = 4


def draw_tile_count(key, part):
    key = jax.random.fold_in(key, 5)
    first_key, second_key = jax.random.split(key)
    counts = jax.random.randint(first_key, (N_ROW * N_COL,), max(1, TILES // 4), TILES + 1)
    chosen = jax.random.randint(second_key, (), 0, N_ROW * N_COL)
    counts = jnp.where(jnp.arange(N_ROW * N_COL) == chosen, TILES, counts)
    return counts.reshape(N_ROW, N_COL).astype(jnp.int32)


def with_ends(drawn, key, least, top_value):
    longest = drawn.shape.index(max(drawn.shape))
    spots = []
    for shift in (0, 1):
        where = [jax.random.randint(jax.random.fold_in(key, axis), (), 0, length) for axis, length in enumerate(drawn.shape)]
        where[longest] = (where[longest] + shift) % drawn.shape[longest]
        spots.append(tuple(where))
    return drawn.at[spots[0]].set(least).at[spots[1]].set(top_value)


def block_scale(key, dims, cuts, low, high):
    level = 1.0
    for dim, parts in cuts:
        heights = jax.random.uniform(jax.random.fold_in(jax.random.fold_in(key, 6), dim), (parts,), jnp.float32, low / len(cuts), high / len(cuts))
        level = level * jnp.repeat(jnp.exp(heights), dims[dim] // parts).reshape((-1,) + (1,) * (len(dims) - 1 - dim))
    return level


def rank_table(amount, lean):
    portions = [(1 << 20) // math.isqrt(grade ** lean) + 1 for grade in range(1, amount + 1)]
    spread = 1 + sum(portions) // (1 << 30)
    return np.cumsum(np.array([max(1, weight // spread) for weight in portions]))


def skewed_ids(own_key, dims, number_of, skew):
    table = rank_table(number_of, skew)
    lot = jax.random.randint(jax.random.fold_in(own_key, 1), dims, 0, int(table[number_of - 1]))
    rank = jnp.searchsorted(jnp.asarray(table, jnp.int32), lot, side="right")
    return jax.random.permutation(jax.random.fold_in(own_key, 2), number_of)[rank].astype(jnp.int32)


def centred(rng, shape, deviation, limit, cuts=(), kind=jnp.bfloat16):
    array = jax.random.normal(rng, shape, jnp.float32) * deviation
    if len(cuts) > 0:
        array = block_scale(rng, shape, cuts, -0.22, 0.18) * array
    return jnp.clip(array, min=-limit, max=limit).astype(kind)


def setup_inputs(seed: int = 0, part: int = 0) -> dict:
    key_list = jax.random.split(jax.random.key(seed), 9)
    part_keys = jax.random.split(jax.random.fold_in(key_list[8], part), 9)
    return {
        "features": centred(part_keys[0], (N_COL, N_ROW, ROWS_DEV, FEAT), 1.0, 6.0, ((0, 4), (1, 4))),
        "weight": centred(key_list[1], (FEAT, FEAT), FEAT ** -0.5, 0.375),
        "bias": centred(key_list[2], (FEAT,), 0.5, 3.0, (), jnp.float32),
        "tile_rows": with_ends(skewed_ids(part_keys[3], (N_ROW, N_COL, TILES), TILE_ROWS, 2), jax.random.fold_in(part_keys[3], 3), 0, TILE_ROWS - 1).astype(jnp.int32),
        "tile_cols": with_ends(jax.random.randint(part_keys[4], (N_ROW, N_COL, TILES), 0, TILE_ROWS), jax.random.fold_in(part_keys[4], 1), 0, TILE_ROWS - 1).astype(jnp.int32),
        "tile_vals": centred(part_keys[5], (N_ROW, N_COL, TILES, TILE, TILE), (TILES * TILE * TILE // ROWS_DEV) ** -0.5, 0.0625, ((0, 4), (1, 4))),
        "tile_count": draw_tile_count(jax.random.fold_in(jax.random.fold_in(key_list[8], part), 71), part),
        "cotangent": centred(part_keys[7], (N_ROW, N_COL, ROWS_DEV, FEAT), 1.0, 6.0, ((0, 4), (1, 4))),
    }


def block_product(values, source_idx, target_idx, live_count, source, forward):
    picked = jnp.take(source, source_idx, axis=0).astype(jnp.float32)
    values32 = values.astype(jnp.float32)
    if forward:
        terms = jnp.einsum("tij,tjf->tif", values32, picked)
    else:
        terms = jnp.einsum("tji,tjf->tif", values32, picked)
    alive = (jnp.arange(values.shape[0], dtype=jnp.int32) < live_count).astype(jnp.float32)
    terms = terms * alive[:, None, None]
    return jax.ops.segment_sum(terms, target_idx, num_segments=source.shape[0])


def reference(features, weight, bias, tile_rows, tile_cols, tile_vals, tile_count, cotangent):
    def forward_row(row_index):
        def one_block(col_index):
            source = features[col_index].reshape(TILE_ROWS, TILE, FEAT)
            term = block_product(tile_vals[row_index, col_index], tile_cols[row_index, col_index],
                                 tile_rows[row_index, col_index], tile_count[row_index, col_index], source, True)
            return term.astype(jnp.bfloat16)
        terms = lax.map(one_block, jnp.arange(N_COL, dtype=jnp.int32))
        summed = jnp.sum(terms.astype(jnp.float32), axis=0).astype(jnp.bfloat16)
        return summed.reshape(N_COL, ROWS_DEV, FEAT)

    aggregated = lax.map(forward_row, jnp.arange(N_ROW, dtype=jnp.int32))
    flat = aggregated.reshape(-1, FEAT)
    pre = jnp.dot(flat, weight, preferred_element_type=jnp.float32) + bias
    hidden = jax.nn.silu(pre).astype(jnp.bfloat16)
    sigma = jax.nn.sigmoid(pre)
    slope = sigma * (1.0 + pre * (1.0 - sigma))
    grad_pre = (cotangent.reshape(-1, FEAT).astype(jnp.float32) * slope).astype(jnp.bfloat16)
    factor = float(NODES) ** -0.5
    grad_weight = jnp.dot(flat.T, grad_pre, preferred_element_type=jnp.float32) * factor
    grad_bias = jnp.sum(grad_pre.astype(jnp.float32), axis=0) * factor
    grad_agg = jnp.dot(grad_pre, weight.T, preferred_element_type=jnp.float32).astype(jnp.bfloat16)
    grad_rows = grad_agg.reshape(N_ROW, TILE_ROWS, TILE, FEAT)

    def backward_col(col_index):
        def one_block(row_index):
            term = block_product(tile_vals[row_index, col_index], tile_rows[row_index, col_index],
                                 tile_cols[row_index, col_index], tile_count[row_index, col_index],
                                 grad_rows[row_index], False)
            return term.astype(jnp.bfloat16)
        terms = lax.map(one_block, jnp.arange(N_ROW, dtype=jnp.int32))
        summed = jnp.sum(terms.astype(jnp.float32), axis=0).astype(jnp.bfloat16)
        return summed.reshape(N_ROW, ROWS_DEV, FEAT)

    grad_features = lax.map(backward_col, jnp.arange(N_COL, dtype=jnp.int32))
    return (hidden.reshape(N_ROW, N_COL, ROWS_DEV, FEAT), grad_features, grad_weight, grad_bias)
```

```python
import functools

import jax
import jax.numpy as jnp
from jax import lax
from jax.experimental import pallas as pl
from jax.experimental.pallas import tpu as pltpu
from jax.sharding import PartitionSpec as P

BF = jnp.bfloat16
F32 = jnp.float32
VMEM = pl.BlockSpec(memory_space=pltpu.VMEM)
SMEM = pl.BlockSpec(memory_space=pltpu.SMEM)


def tile_terms(values, picked, forward):
    if forward:
        return jnp.einsum("tij,tjf->tif", values, picked, preferred_element_type=jnp.float32)
    return jnp.einsum("tji,tjf->tif", values, picked, preferred_element_type=jnp.float32)


def every_slot(values, source_idx, target_idx, live_count, source, forward):
    width = min(16, values.shape[0])
    targets = source.shape[0]

    def advance(index, carry):
        start = index * width
        block_values = lax.dynamic_slice_in_dim(values, start, width, 0)
        block_source = lax.dynamic_slice_in_dim(source_idx, start, width, 0)
        block_target = lax.dynamic_slice_in_dim(target_idx, start, width, 0)
        picked = jnp.take(source, block_source, axis=0)
        terms = tile_terms(block_values, picked, forward)
        alive_mask = (start + jnp.arange(width) < live_count).astype(jnp.float32)
        placing = (jnp.arange(targets)[:, None] == block_target[None, :]).astype(jnp.float32)
        placing = placing * alive_mask[None, :]
        added = jnp.einsum("rt,tif->rif", placing, terms, precision=lax.Precision.HIGHEST)
        return carry + added

    initial = jnp.zeros(source.shape, jnp.float32)
    return lax.fori_loop(0, values.shape[0] // width, advance, initial)


def sparse_device(features, weight, bias, tile_rows, tile_cols, tile_vals, tile_count, cotangent):
    own_rows = features[0, 0]
    rows_dev, feat = own_rows.shape
    tile = tile_vals.shape[-1]
    values = tile_vals[0, 0]
    row_idx = tile_rows[0, 0]
    col_idx = tile_cols[0, 0]
    live_count = tile_count[0, 0]
    gathered = lax.all_gather(own_rows, "row", axis=0, tiled=True)
    block_nodes = gathered.shape[0]
    source = gathered.reshape(block_nodes // tile, tile, feat)
    forward_terms = every_slot(values, col_idx, row_idx, live_count, source, True)
    summed = lax.psum_scatter(
        forward_terms.reshape(block_nodes, feat).astype(BF), "col", scatter_dimension=0, tiled=True
    )
    pre = jnp.dot(summed, weight, preferred_element_type=F32) + bias
    hidden = jax.nn.silu(pre).astype(BF)
    sigma = jax.nn.sigmoid(pre)
    slope = sigma * (1.0 + pre * (1.0 - sigma))
    grad_pre = (cotangent[0, 0].astype(F32) * slope).astype(BF)
    weight_term = lax.dot_general(
        summed, grad_pre, (((0,), (0,)), ((), ())), preferred_element_type=F32
    )
    bias_term = jnp.sum(grad_pre.astype(F32), axis=0)
    weight_sum, bias_sum = lax.psum((weight_term, bias_term), ("row", "col"))
    node_total = rows_dev * lax.axis_size("row") * lax.axis_size("col")
    factor = float(node_total) ** (-0.5)
    grad_local = jnp.dot(grad_pre, weight.T, preferred_element_type=F32).astype(BF)
    grad_rows = lax.all_gather(grad_local, "col", axis=0, tiled=True)
    grad_source = grad_rows.reshape(block_nodes // tile, tile, feat)
    backward_terms = every_slot(values, row_idx, col_idx, live_count, grad_source, False)
    back_summed = lax.psum_scatter(
        backward_terms.reshape(block_nodes, feat).astype(BF), "row", scatter_dimension=0, tiled=True
    )
    hidden_out = hidden.reshape(1, 1, rows_dev, feat)
    grad_features = back_summed.reshape(1, 1, rows_dev, feat)
    return (hidden_out, grad_features, weight_sum * factor, bias_sum * factor)


def swap(x, axis, bit):
    size = lax.axis_size(axis)
    return lax.ppermute(x, axis, [(i, i ^ bit) for i in range(size)])


def build_kernel(rows_ref, cols_ref, count_ref, vals_ref, dense_ref, total):
    step = pl.program_id(0)
    width, tile, _ = vals_ref.shape
    wide, nodes, _ = total.shape
    per = dense_ref.shape[2] // tile

    @pl.when(step == 0)
    def _():
        total[...] = jnp.zeros_like(total)

    def place(slot, carry):
        row = rows_ref[step * width + slot]
        col = cols_ref[step * width + slot]
        where = pl.ds(pl.multiple_of(row * tile, tile), tile)
        total[col, where, :] += vals_ref[slot].astype(F32)
        return carry

    lax.fori_loop(0, jnp.clip(count_ref[0] - step * width, 0, width), place, 0)

    @pl.when(step == pl.num_programs(0) - 1)
    def _():
        for col in range(wide):
            dense_ref[col // per, :, (col % per) * tile : (col % per + 1) * tile] = total[col].astype(BF)


def build_dense(values, row_idx, col_idx, count, parts, rows_dev):
    slots, tile, _ = values.shape
    nodes = parts * rows_dev
    width = 16

    def live_block(step, rows, cols, live):
        return (jnp.minimum(step, jnp.maximum(live[0] - 1, 0) // width), 0, 0)

    return pl.pallas_call(
        build_kernel,
        grid_spec=pltpu.PrefetchScalarGridSpec(
            num_scalar_prefetch=3,
            grid=(slots // width,),
            in_specs=[pl.BlockSpec((width, tile, tile), live_block)],
            out_specs=pl.BlockSpec((parts, nodes, rows_dev), lambda *_: (0, 0, 0)),
            scratch_shapes=[pltpu.VMEM((nodes // tile, nodes, tile), F32)],
        ),
        out_shape=jax.ShapeDtypeStruct((parts, nodes, rows_dev), BF),
        compiler_params=pltpu.CompilerParams(vmem_limit_bytes=32 << 20),
        cost_estimate=pl.CostEstimate(flops=8 * nodes * nodes, bytes_accessed=6 * nodes * nodes, transcendentals=0),
        name="build_dense",
    )(row_idx, col_idx, count, values)


def forward_kernel(place_ref, dense_ref, *refs):
    parts = dense_ref.shape[0]
    sources, outs = refs[:parts], refs[parts:]
    rows = sources[0].shape[0]
    row, col = place_ref[0], place_ref[1]
    for k in range(parts):
        where = pl.ds(pl.multiple_of((col ^ k) * rows, rows), rows)
        total = None
        for j in range(parts):
            term = jnp.dot(dense_ref[row ^ j, where, :], sources[j][...], preferred_element_type=F32)
            total = term if total is None else total + term
        outs[k][...] = total.astype(BF)


def backward_kernel(place_ref, dense_ref, *refs):
    parts = dense_ref.shape[0]
    sources, outs = refs[:parts], refs[parts:]
    rows = sources[0].shape[0]
    row, col = place_ref[0], place_ref[1]
    for k in range(parts):
        total = None
        for j in range(parts):
            where = pl.ds(pl.multiple_of((col ^ j) * rows, rows), rows)
            term = lax.dot_general(
                dense_ref[row ^ k, where, :], sources[j][...], (((0,), (0,)), ((), ())),
                preferred_element_type=F32,
            )
            total = term if total is None else total + term
        outs[k][...] = total.astype(BF)


def product(kernel, name, place, dense, sources):
    parts = len(sources)
    rows, feat = sources[0].shape
    return pl.pallas_call(
        kernel,
        in_specs=[SMEM] + [VMEM] * (1 + parts),
        out_specs=[VMEM] * parts,
        out_shape=[jax.ShapeDtypeStruct((rows, feat), BF)] * parts,
        compiler_params=pltpu.CompilerParams(vmem_limit_bytes=32 << 20),
        cost_estimate=pl.CostEstimate(
            flops=2 * parts * parts * rows * rows * feat,
            bytes_accessed=2 * parts * rows * (parts * rows + 2 * feat),
            transcendentals=0,
        ),
        name=name,
    )(place, dense, *sources)


def layer_kernel(weight_ref, bias_ref, cot_ref, *refs):
    terms, (hidden_ref, agg_ref, wgrad_ref, bgrad_ref) = refs[:-4], refs[-4:]
    summed = terms[0][...].astype(F32)
    for term in terms[1:]:
        summed = summed + term[...].astype(F32)
    summed = summed.astype(BF)
    pre = jnp.dot(summed, weight_ref[...], preferred_element_type=F32) + bias_ref[...]
    sigma = jax.nn.sigmoid(pre)
    hidden_ref[...] = (pre * sigma).astype(BF)
    slope = sigma * (1.0 + pre * (1.0 - sigma))
    grad_pre = (cot_ref[...].astype(F32) * slope).astype(BF)
    agg_ref[...] = lax.dot_general(
        grad_pre, weight_ref[...], (((1,), (1,)), ((), ())), preferred_element_type=F32
    ).astype(BF)
    wgrad_ref[...] = lax.dot_general(
        summed, grad_pre, (((0,), (0,)), ((), ())), preferred_element_type=F32
    )
    bgrad_ref[...] = jnp.sum(grad_pre.astype(F32), axis=0, keepdims=True)


def layer(weight, bias, cot, terms):
    rows, feat = cot.shape
    return pl.pallas_call(
        layer_kernel,
        in_specs=[VMEM] * (3 + len(terms)),
        out_specs=[VMEM] * 4,
        out_shape=[
            jax.ShapeDtypeStruct((rows, feat), BF),
            jax.ShapeDtypeStruct((rows, feat), BF),
            jax.ShapeDtypeStruct((feat, feat), F32),
            jax.ShapeDtypeStruct((1, feat), F32),
        ],
        cost_estimate=pl.CostEstimate(
            flops=6 * rows * feat * feat, bytes_accessed=20 * rows * feat, transcendentals=rows * feat
        ),
        name="layer",
    )(weight, bias, cot, *terms)


def dense_device(features, weight, bias, tile_rows, tile_cols, tile_vals, tile_count, cotangent):
    own = features[0, 0]
    rows, feat = own.shape
    row, col = lax.axis_index("row"), lax.axis_index("col")
    place = jnp.stack([row, col]).astype(jnp.int32)

    from_chip = swap(own, "row", 2)
    from_core = swap(own, "row", 1)
    dense = build_dense(tile_vals[0, 0], tile_rows[0, 0], tile_cols[0, 0], tile_count[0], 4, rows)
    sources = [own, from_core, from_chip, swap(from_chip, "row", 1)]
    partial = product(forward_kernel, "forward", place, dense, sources)

    terms = [partial[0]] + [swap(partial[k], "col", k) for k in (2, 3, 1)]
    hidden, agg, wgrad, bgrad = layer(weight, bias[None, :], cotangent[0, 0], terms)

    grads = {0: agg}
    for k in (2, 3, 1):
        grads[k] = swap(agg, "col", k)

    packed = jnp.concatenate([wgrad, jnp.broadcast_to(bgrad, (16, feat))], axis=0)
    packed = packed + swap(packed, "row", 1)
    height = packed.shape[0] // 2
    half = lax.dynamic_slice_in_dim(packed, (row % 2) * height, height, 0)
    half = half + swap(half, "row", 2)

    back = product(backward_kernel, "backward", place, dense, [grads[k] for k in range(4)])

    arrived = swap(jnp.stack([back[1], back[3]]), "row", 1)
    keep = back[0].astype(F32) + arrived[0].astype(F32)
    send = (back[2].astype(F32) + arrived[1].astype(F32)).astype(BF)
    other = swap(send, "row", 2)

    pieces = [swap(half, "col", k) for k in (2, 3, 1)]
    half = half + pieces[0] + pieces[1] + pieces[2]
    twin = swap(half, "row", 1)
    first = row % 2 == 0
    whole = jnp.concatenate([jnp.where(first, half, twin), jnp.where(first, twin, half)], axis=0)
    factor = float(rows * 16) ** (-0.5)

    grad_features = (keep + other.astype(F32)).astype(BF)
    return (
        hidden[None, None],
        grad_features[None, None],
        whole[:feat] * factor,
        whole[feat] * factor,
    )


def per_device(features, weight, bias, tile_rows, tile_cols, tile_vals, tile_count, cotangent):
    rows = features.shape[2]
    slots, tile, _ = tile_vals.shape[2:]
    square = lax.axis_size("row") == 4 and lax.axis_size("col") == 4
    dense_fits = (4 * rows // tile) ** 2 <= slots
    chosen = dense_device if square and dense_fits else sparse_device
    return chosen(features, weight, bias, tile_rows, tile_cols, tile_vals, tile_count, cotangent)


def solution(mesh):
    placed = (
        P(("groups", "col"), "row", None, None),
        P(),
        P(),
        P(("groups", "row"), "col", None),
        P(("groups", "row"), "col", None),
        P(("groups", "row"), "col", None, None, None),
        P(("groups", "row"), "col"),
        P(("groups", "row"), "col", None, None),
    )
    return jax.shard_map(
        per_device,
        mesh=mesh,
        in_specs=placed,
        out_specs=(
            P(("groups", "row"), "col", None, None),
            P(("groups", "col"), "row", None, None),
            P("groups", None),
            P("groups"),
        ),
        check_vma=False,
    )
```

```python
import functools

import jax
import jax.numpy as jnp
from jax import lax
from jax.experimental import pallas as pl
from jax.experimental.pallas import tpu as pltpu
from jax.sharding import PartitionSpec as P

BF = jnp.bfloat16
F32 = jnp.float32
VMEM = pl.BlockSpec(memory_space=pltpu.VMEM)
HBM = pl.BlockSpec(memory_space=pltpu.HBM)
PIECES = 1


def tile_terms(values, picked, forward):
    if forward:
        return jnp.einsum("tij,tjf->tif", values, picked, preferred_element_type=jnp.float32)
    return jnp.einsum("tji,tjf->tif", values, picked, preferred_element_type=jnp.float32)


def every_slot(values, source_idx, target_idx, live_count, source, forward):
    width = min(16, values.shape[0])
    targets = source.shape[0]

    def advance(index, carry):
        start = index * width
        block_values = lax.dynamic_slice_in_dim(values, start, width, 0)
        block_source = lax.dynamic_slice_in_dim(source_idx, start, width, 0)
        block_target = lax.dynamic_slice_in_dim(target_idx, start, width, 0)
        picked = jnp.take(source, block_source, axis=0)
        terms = tile_terms(block_values, picked, forward)
        alive_mask = (start + jnp.arange(width) < live_count).astype(jnp.float32)
        placing = (jnp.arange(targets)[:, None] == block_target[None, :]).astype(jnp.float32)
        placing = placing * alive_mask[None, :]
        added = jnp.einsum("rt,tif->rif", placing, terms, precision=lax.Precision.HIGHEST)
        return carry + added

    initial = jnp.zeros(source.shape, jnp.float32)
    return lax.fori_loop(0, values.shape[0] // width, advance, initial)


def sparse_device(features, weight, bias, tile_rows, tile_cols, tile_vals, tile_count, cotangent):
    own_rows = features[0, 0]
    rows_dev, feat = own_rows.shape
    tile = tile_vals.shape[-1]
    values = tile_vals[0, 0]
    row_idx = tile_rows[0, 0]
    col_idx = tile_cols[0, 0]
    live_count = tile_count[0, 0]
    gathered = lax.all_gather(own_rows, "row", axis=0, tiled=True)
    block_nodes = gathered.shape[0]
    source = gathered.reshape(block_nodes // tile, tile, feat)
    forward_terms = every_slot(values, col_idx, row_idx, live_count, source, True)
    summed = lax.psum_scatter(
        forward_terms.reshape(block_nodes, feat).astype(BF), "col", scatter_dimension=0, tiled=True
    )
    pre = jnp.dot(summed, weight, preferred_element_type=F32) + bias
    hidden = jax.nn.silu(pre).astype(BF)
    sigma = jax.nn.sigmoid(pre)
    slope = sigma * (1.0 + pre * (1.0 - sigma))
    grad_pre = (cotangent[0, 0].astype(F32) * slope).astype(BF)
    weight_term = lax.dot_general(
        summed, grad_pre, (((0,), (0,)), ((), ())), preferred_element_type=F32
    )
    bias_term = jnp.sum(grad_pre.astype(F32), axis=0)
    weight_sum, bias_sum = lax.psum((weight_term, bias_term), ("row", "col"))
    node_total = rows_dev * lax.axis_size("row") * lax.axis_size("col")
    factor = float(node_total) ** (-0.5)
    grad_local = jnp.dot(grad_pre, weight.T, preferred_element_type=F32).astype(BF)
    grad_rows = lax.all_gather(grad_local, "col", axis=0, tiled=True)
    grad_source = grad_rows.reshape(block_nodes // tile, tile, feat)
    backward_terms = every_slot(values, row_idx, col_idx, live_count, grad_source, False)
    back_summed = lax.psum_scatter(
        backward_terms.reshape(block_nodes, feat).astype(BF), "row", scatter_dimension=0, tiled=True
    )
    hidden_out = hidden.reshape(1, 1, rows_dev, feat)
    grad_features = back_summed.reshape(1, 1, rows_dev, feat)
    return (hidden_out, grad_features, weight_sum * factor, bias_sum * factor)


def swap(x, axis, bit):
    size = lax.axis_size(axis)
    return lax.ppermute(x, axis, [(i, i ^ bit) for i in range(size)])


def tree(own, near, far, cross):
    own, near, far, cross = (x.astype(F32) for x in (own, near, far, cross))
    return (own + near) + (far + cross)


def build_kernel(slots_hbm, vals_hbm, dense_ref, slots_ref, vals_ref, total, sem):
    slots, tile, _ = vals_ref.shape
    chunks = sem.shape[0] - 1
    width = slots // chunks
    per = dense_ref.shape[2] // tile
    wide = total.shape[0]
    small = pltpu.make_async_copy(slots_hbm, slots_ref, sem.at[chunks])
    big = [
        pltpu.make_async_copy(
            vals_hbm.at[pl.ds(i * width, width)], vals_ref.at[pl.ds(i * width, width)], sem.at[i]
        )
        for i in range(chunks)
    ]
    small.start()
    for copy in big:
        copy.start()
    total[...] = jnp.zeros_like(total)
    small.wait()
    live = slots_ref[slots]

    def place(slot, carry):
        spot = slots_ref[slot]
        where = pl.ds(pl.multiple_of(lax.div(spot, wide) * tile, tile), tile)
        total[lax.rem(spot, wide), where, :] += vals_ref[slot].astype(F32)
        return carry

    for i in range(chunks):
        big[i].wait()
        lax.fori_loop(i * width, jnp.clip(live, i * width, (i + 1) * width), place, 0)

    for col in range(wide):
        dense_ref[col // per, :, (col % per) * tile : (col % per + 1) * tile] = total[col].astype(BF)


def build_dense(values, row_idx, col_idx, count, parts, rows_dev):
    slots, tile, _ = values.shape
    nodes = parts * rows_dev
    wide = nodes // tile
    chunks = 8
    listed = jnp.concatenate([row_idx * wide + col_idx, jnp.broadcast_to(count, (slots,))])
    return pl.pallas_call(
        build_kernel,
        in_specs=[HBM] * 2,
        out_specs=VMEM,
        out_shape=jax.ShapeDtypeStruct((parts, nodes, rows_dev), BF),
        scratch_shapes=[
            pltpu.SMEM(listed.shape, jnp.int32),
            pltpu.VMEM(values.shape, BF),
            pltpu.VMEM((wide, nodes, tile), F32),
            pltpu.SemaphoreType.DMA((chunks + 1,)),
        ],
        compiler_params=pltpu.CompilerParams(vmem_limit_bytes=50 << 20),
        cost_estimate=pl.CostEstimate(flops=8 * nodes * nodes, bytes_accessed=6 * nodes * nodes, transcendentals=0),
        name="build_dense",
    )(listed, values)


def forward_kernel(dense_ref, *refs):
    parts = dense_ref.shape[0]
    sources, outs = refs[:parts], refs[parts:]
    rows = sources[0].shape[0]
    row, col = lax.axis_index("row"), lax.axis_index("col")
    for k in range(parts):
        where = pl.ds(pl.multiple_of((col ^ k) * rows, rows), rows)
        total = None
        for j in range(parts):
            term = jnp.dot(dense_ref[row ^ j, where, :], sources[j][...], preferred_element_type=F32)
            total = term if total is None else total + term
        total = total.astype(BF)
        for h in range(PIECES):
            height = rows // PIECES
            outs[h * parts + k][...] = total[h * height : (h + 1) * height]


def forward(dense, sources):
    parts = len(sources)
    rows, feat = sources[0].shape
    return pl.pallas_call(
        forward_kernel,
        in_specs=[VMEM] * (1 + parts),
        out_specs=[VMEM] * (parts * PIECES),
        out_shape=[jax.ShapeDtypeStruct((rows // PIECES, feat), BF)] * (parts * PIECES),
        compiler_params=pltpu.CompilerParams(vmem_limit_bytes=8 << 20),
        cost_estimate=product_cost(parts, rows, feat),
        name="forward",
    )(dense, *sources)


def product_cost(parts, rows, feat):
    return pl.CostEstimate(
        flops=2 * parts * parts * rows * rows * feat,
        bytes_accessed=2 * parts * rows * (parts * rows + 2 * feat),
        transcendentals=0,
    )


def backward_kernel(dense_ref, *refs):
    parts = dense_ref.shape[0]
    sources, refs = refs[: parts * PIECES], refs[parts * PIECES :]
    keep_refs, pair_ref = refs[:2], refs[2]
    rows = sources[0].shape[0] * PIECES
    row, col = lax.axis_index("row"), lax.axis_index("col")
    for k in (1, 3, 0, 2):
        total = None
        for j in range(parts):
            where = pl.ds(pl.multiple_of((col ^ j) * rows, rows), rows)
            source = jnp.concatenate([sources[h * parts + j][...] for h in range(PIECES)], axis=0)
            term = lax.dot_general(
                dense_ref[row ^ k, where, :], source, (((0,), (0,)), ((), ())),
                preferred_element_type=F32,
            )
            total = term if total is None else total + term
        if k % 2:
            pair_ref[k // 2] = total.astype(BF)
        else:
            keep_refs[k // 2][...] = total


def backward(dense, sources):
    parts = len(sources) // PIECES
    rows, feat = sources[0].shape[0] * PIECES, sources[0].shape[1]
    return pl.pallas_call(
        backward_kernel,
        in_specs=[VMEM] * (1 + parts * PIECES),
        out_specs=[VMEM] * 3,
        out_shape=[
            jax.ShapeDtypeStruct((rows, feat), F32),
            jax.ShapeDtypeStruct((rows, feat), F32),
            jax.ShapeDtypeStruct((2, rows, feat), BF),
        ],
        compiler_params=pltpu.CompilerParams(vmem_limit_bytes=8 << 20),
        cost_estimate=product_cost(parts, rows, feat),
        name="backward",
    )(dense, *sources)


def pair_kernel(keep_ref, send_ref, arrived_ref, kept_ref, sent_ref):
    kept_ref[...] = keep_ref[...] + arrived_ref[0].astype(F32)
    sent_ref[...] = (send_ref[...] + arrived_ref[1].astype(F32)).astype(BF)


def pair_sum(keep, send, arrived):
    return pl.pallas_call(
        pair_kernel,
        in_specs=[VMEM] * 3,
        out_specs=[VMEM] * 2,
        out_shape=[
            jax.ShapeDtypeStruct(keep.shape, F32),
            jax.ShapeDtypeStruct(send.shape, BF),
        ],
        compiler_params=pltpu.CompilerParams(vmem_limit_bytes=8 << 20),
        cost_estimate=pl.CostEstimate(flops=3 * keep.size, bytes_accessed=20 * keep.size, transcendentals=0),
        name="pair_sum",
    )(keep, send, arrived)


def gradient_kernel(weight_ref, bias_ref, cot_ref, *refs):
    refs, (agg_ref, summed_ref, pre_ref, grad_ref) = refs[:-4], refs[-4:]
    terms = refs[:4]
    summed = terms[0][...].astype(F32)
    for term in terms[1:]:
        summed = summed + term[...].astype(F32)
    summed = summed.astype(BF)
    summed_ref[...] = summed
    pre = jnp.dot(summed, weight_ref[...], preferred_element_type=F32) + bias_ref[...]
    pre_ref[...] = pre
    sigma = jax.nn.sigmoid(pre)
    slope = sigma * (1.0 + pre * (1.0 - sigma))
    grad_pre = (cot_ref[...].astype(F32) * slope).astype(BF)
    grad_ref[...] = grad_pre
    agg_ref[...] = lax.dot_general(
        grad_pre, weight_ref[...], (((1,), (1,)), ((), ())), preferred_element_type=F32
    ).astype(BF)


def gradient(weight, bias, cot, terms, after, piece):
    rows, feat = terms[0].shape
    block = jax.ShapeDtypeStruct((rows, feat), BF)
    return pl.pallas_call(
        gradient_kernel,
        grid=(1,),
        in_specs=[VMEM, VMEM, pl.BlockSpec((rows, feat), lambda _: (piece, 0))]
        + [VMEM] * (len(terms) + len(after)),
        out_specs=[VMEM] * 4,
        out_shape=[block, block, jax.ShapeDtypeStruct((rows, feat), F32), block],
        compiler_params=pltpu.CompilerParams(vmem_limit_bytes=8 << 20),
        cost_estimate=pl.CostEstimate(
            flops=4 * rows * feat * feat, bytes_accessed=20 * rows * feat, transcendentals=rows * feat
        ),
        name="gradient",
    )(weight, bias, cot, *terms, *after)


def totals_kernel(after_ref, *refs):
    del after_ref
    summed_refs, pre_refs, grad_refs = (refs[i * PIECES : (i + 1) * PIECES] for i in range(3))
    hidden_ref, mine_ref, other_ref = refs[3 * PIECES :]
    height, feat = summed_refs[0].shape
    core = lax.axis_index("row") & 1
    for h in range(PIECES):
        pre = pre_refs[h][...]
        hidden_ref[h * height : (h + 1) * height, :] = (pre * jax.nn.sigmoid(pre)).astype(BF)
    grad_pre = jnp.concatenate([ref[...] for ref in grad_refs], axis=0)
    bias_row = jnp.sum(grad_pre.astype(F32), axis=0, keepdims=True)
    middle = feat // 2
    for target, index in ((mine_ref, core), (other_ref, 1 - core)):
        window = pl.ds(pl.multiple_of(index * middle, middle), middle)
        columns = jnp.concatenate([ref[:, window] for ref in summed_refs], axis=0)
        product = lax.dot_general(columns, grad_pre, (((0,), (0,)), ((), ())), preferred_element_type=F32)
        spread = jnp.broadcast_to(bias_row, (mine_ref.shape[0] - middle, feat))
        target[:middle, :] = product.astype(BF)
        target[middle:, :] = spread.astype(BF)


def totals(after, summed, pre, grad_pre):
    rows, feat = pre[0].shape[0] * PIECES, pre[0].shape[1]
    half = (feat // 2 + 16, feat)
    return pl.pallas_call(
        totals_kernel,
        in_specs=[VMEM] * (1 + 3 * PIECES),
        out_specs=[VMEM] * 3,
        out_shape=[
            jax.ShapeDtypeStruct((rows, feat), BF),
            jax.ShapeDtypeStruct(half, BF),
            jax.ShapeDtypeStruct(half, BF),
        ],
        compiler_params=pltpu.CompilerParams(vmem_limit_bytes=8 << 20),
        cost_estimate=pl.CostEstimate(
            flops=2 * rows * feat * feat, bytes_accessed=20 * rows * feat, transcendentals=rows * feat
        ),
        name="totals",
    )(after, *summed, *pre, *grad_pre)


def dense_device(features, weight, bias, tile_rows, tile_cols, tile_vals, tile_count, cotangent):
    own = features[0, 0]
    rows, feat = own.shape
    row = lax.axis_index("row")

    from_chip = swap(own, "row", 2)
    from_core = swap(own, "row", 1)
    dense = build_dense(tile_vals[0, 0], tile_rows[0, 0], tile_cols[0, 0], tile_count[0], 4, rows)
    dense, from_chip = lax.optimization_barrier((dense, from_chip))
    sources = [own, from_core, from_chip, swap(from_chip, "row", 1)]
    partial = forward(dense, sources)

    kept, gathered, after = [], [], []
    for h in range(PIECES):
        mine = partial[h * 4 : (h + 1) * 4]
        terms = [mine[0]] + [swap(mine[k], "col", k) for k in (2, 3, 1)]
        agg, *rest = gradient(weight, bias[None, :], cotangent[0, 0], terms, after, h)
        kept.append(rest)
        after = [agg]
        early = swap(agg, "col", 1)
        grads = {0: agg, 1: early}
        grads[2] = swap(agg, "col", 2)
        grads[3] = swap(grads[2], "col", 1)
        gathered += [grads[k] for k in range(4)]

    hidden, mine, others = totals(agg, *zip(*kept))
    half = tree(mine, swap(others, "row", 1), swap(mine, "row", 2), swap(others, "row", 3)).astype(BF)

    keep, send, pair = backward(dense, gathered)
    keep, send = pair_sum(keep, send, swap(pair, "row", 1))
    grad_features = (keep + swap(send, "row", 2).astype(F32)).astype(BF)

    half = tree(half, *(swap(half, "col", k) for k in (1, 2, 3)))
    twin = swap(half, "row", 1)
    first = row % 2 == 0
    middle = feat // 2
    factor = float(rows * 16) ** (-0.5)
    low, high = jnp.where(first, half, twin), jnp.where(first, twin, half)
    grad_weight = jnp.concatenate([low[:middle], high[:middle]], axis=0) * factor
    return (hidden[None, None], grad_features[None, None], grad_weight, half[middle] * factor)


def per_device(features, weight, bias, tile_rows, tile_cols, tile_vals, tile_count, cotangent):
    rows = features.shape[2]
    slots, tile, _ = tile_vals.shape[2:]
    square = lax.axis_size("row") == 4 and lax.axis_size("col") == 4
    dense_fits = (4 * rows // tile) ** 2 <= slots
    chosen = dense_device if square and dense_fits else sparse_device
    return chosen(features, weight, bias, tile_rows, tile_cols, tile_vals, tile_count, cotangent)


def solution(mesh):
    placed = (
        P(("groups", "col"), "row", None, None),
        P(),
        P(),
        P(("groups", "row"), "col", None),
        P(("groups", "row"), "col", None),
        P(("groups", "row"), "col", None, None, None),
        P(("groups", "row"), "col"),
        P(("groups", "row"), "col", None, None),
    )
    return jax.shard_map(
        per_device,
        mesh=mesh,
        in_specs=placed,
        out_specs=(
            P(("groups", "row"), "col", None, None),
            P(("groups", "col"), "row", None, None),
            P("groups", None),
            P("groups"),
        ),
        check_vma=False,
    )
```

```python
import functools

import jax
import jax.numpy as jnp
from jax import lax
from jax.experimental import pallas as pl
from jax.experimental.pallas import tpu as pltpu
from jax.sharding import PartitionSpec as P

BF = jnp.bfloat16
F32 = jnp.float32
VMEM = pl.BlockSpec(memory_space=pltpu.VMEM)
HBM = pl.BlockSpec(memory_space=pltpu.HBM)
PIECES = 1


def tile_terms(values, picked, forward):
    if forward:
        return jnp.einsum("tij,tjf->tif", values, picked, preferred_element_type=jnp.float32)
    return jnp.einsum("tji,tjf->tif", values, picked, preferred_element_type=jnp.float32)


def every_slot(values, source_idx, target_idx, live_count, source, forward):
    width = min(16, values.shape[0])
    targets = source.shape[0]

    def advance(index, carry):
        start = index * width
        block_values = lax.dynamic_slice_in_dim(values, start, width, 0)
        block_source = lax.dynamic_slice_in_dim(source_idx, start, width, 0)
        block_target = lax.dynamic_slice_in_dim(target_idx, start, width, 0)
        picked = jnp.take(source, block_source, axis=0)
        terms = tile_terms(block_values, picked, forward)
        alive_mask = (start + jnp.arange(width) < live_count).astype(jnp.float32)
        placing = (jnp.arange(targets)[:, None] == block_target[None, :]).astype(jnp.float32)
        placing = placing * alive_mask[None, :]
        added = jnp.einsum("rt,tif->rif", placing, terms, precision=lax.Precision.HIGHEST)
        return carry + added

    initial = jnp.zeros(source.shape, jnp.float32)
    return lax.fori_loop(0, values.shape[0] // width, advance, initial)


def sparse_device(features, weight, bias, tile_rows, tile_cols, tile_vals, tile_count, cotangent):
    own_rows = features[0, 0]
    rows_dev, feat = own_rows.shape
    tile = tile_vals.shape[-1]
    values = tile_vals[0, 0]
    row_idx = tile_rows[0, 0]
    col_idx = tile_cols[0, 0]
    live_count = tile_count[0, 0]
    gathered = lax.all_gather(own_rows, "row", axis=0, tiled=True)
    block_nodes = gathered.shape[0]
    source = gathered.reshape(block_nodes // tile, tile, feat)
    forward_terms = every_slot(values, col_idx, row_idx, live_count, source, True)
    summed = lax.psum_scatter(
        forward_terms.reshape(block_nodes, feat).astype(BF), "col", scatter_dimension=0, tiled=True
    )
    pre = jnp.dot(summed, weight, preferred_element_type=F32) + bias
    hidden = jax.nn.silu(pre).astype(BF)
    sigma = jax.nn.sigmoid(pre)
    slope = sigma * (1.0 + pre * (1.0 - sigma))
    grad_pre = (cotangent[0, 0].astype(F32) * slope).astype(BF)
    weight_term = lax.dot_general(
        summed, grad_pre, (((0,), (0,)), ((), ())), preferred_element_type=F32
    )
    bias_term = jnp.sum(grad_pre.astype(F32), axis=0)
    weight_sum, bias_sum = lax.psum((weight_term, bias_term), ("row", "col"))
    node_total = rows_dev * lax.axis_size("row") * lax.axis_size("col")
    factor = float(node_total) ** (-0.5)
    grad_local = jnp.dot(grad_pre, weight.T, preferred_element_type=F32).astype(BF)
    grad_rows = lax.all_gather(grad_local, "col", axis=0, tiled=True)
    grad_source = grad_rows.reshape(block_nodes // tile, tile, feat)
    backward_terms = every_slot(values, row_idx, col_idx, live_count, grad_source, False)
    back_summed = lax.psum_scatter(
        backward_terms.reshape(block_nodes, feat).astype(BF), "row", scatter_dimension=0, tiled=True
    )
    hidden_out = hidden.reshape(1, 1, rows_dev, feat)
    grad_features = back_summed.reshape(1, 1, rows_dev, feat)
    return (hidden_out, grad_features, weight_sum * factor, bias_sum * factor)


def swap(x, axis, bit):
    size = lax.axis_size(axis)
    return lax.ppermute(x, axis, [(i, i ^ bit) for i in range(size)])


def tree(own, near, far, cross):
    own, near, far, cross = (x.astype(F32) for x in (own, near, far, cross))
    return (own + near) + (far + cross)


def build_kernel(slots_hbm, vals_hbm, dense_ref, slots_ref, vals_ref, total, sem):
    slots, tile, _ = vals_ref.shape
    chunks = sem.shape[0] - 1
    width = slots // chunks
    per = dense_ref.shape[2] // tile
    wide = total.shape[0]
    small = pltpu.make_async_copy(slots_hbm, slots_ref, sem.at[chunks])
    big = [
        pltpu.make_async_copy(
            vals_hbm.at[pl.ds(i * width, width)], vals_ref.at[pl.ds(i * width, width)], sem.at[i]
        )
        for i in range(chunks)
    ]
    small.start()
    for copy in big:
        copy.start()
    total[...] = jnp.zeros_like(total)
    small.wait()
    live = slots_ref[slots]

    def place(slot, carry):
        spot = slots_ref[slot]
        where = pl.ds(pl.multiple_of(lax.div(spot, wide) * tile, tile), tile)
        total[lax.rem(spot, wide), where, :] += vals_ref[slot].astype(F32)
        return carry

    for i in range(chunks):
        big[i].wait()
        lax.fori_loop(i * width, jnp.clip(live, i * width, (i + 1) * width), place, 0)

    for col in range(wide):
        dense_ref[col // per, :, (col % per) * tile : (col % per + 1) * tile] = total[col].astype(BF)


def build_dense(values, row_idx, col_idx, count, parts, rows_dev):
    slots, tile, _ = values.shape
    nodes = parts * rows_dev
    wide = nodes // tile
    chunks = 8
    listed = jnp.concatenate([row_idx * wide + col_idx, jnp.broadcast_to(count, (slots,))])
    return pl.pallas_call(
        build_kernel,
        in_specs=[HBM] * 2,
        out_specs=VMEM,
        out_shape=jax.ShapeDtypeStruct((parts, nodes, rows_dev), BF),
        scratch_shapes=[
            pltpu.SMEM(listed.shape, jnp.int32),
            pltpu.VMEM(values.shape, BF),
            pltpu.VMEM((wide, nodes, tile), F32),
            pltpu.SemaphoreType.DMA((chunks + 1,)),
        ],
        compiler_params=pltpu.CompilerParams(vmem_limit_bytes=50 << 20),
        cost_estimate=pl.CostEstimate(flops=8 * nodes * nodes, bytes_accessed=6 * nodes * nodes, transcendentals=0),
        name="build_dense",
    )(listed, values)


def forward_kernel(dense_ref, *refs):
    parts = dense_ref.shape[0]
    sources, outs = refs[:parts], refs[parts:]
    rows = sources[0].shape[0]
    row, col = lax.axis_index("row"), lax.axis_index("col")
    for k in range(parts):
        where = pl.ds(pl.multiple_of((col ^ k) * rows, rows), rows)
        total = None
        for j in range(parts):
            term = jnp.dot(dense_ref[row ^ j, where, :], sources[j][...], preferred_element_type=F32)
            total = term if total is None else total + term
        total = total.astype(BF)
        for h in range(PIECES):
            height = rows // PIECES
            outs[h * parts + k][...] = total[h * height : (h + 1) * height]


def forward(dense, sources):
    parts = len(sources)
    rows, feat = sources[0].shape
    return pl.pallas_call(
        forward_kernel,
        in_specs=[VMEM] * (1 + parts),
        out_specs=[VMEM] * (parts * PIECES),
        out_shape=[jax.ShapeDtypeStruct((rows // PIECES, feat), BF)] * (parts * PIECES),
        compiler_params=pltpu.CompilerParams(vmem_limit_bytes=8 << 20),
        cost_estimate=product_cost(parts, rows, feat),
        name="forward",
    )(dense, *sources)


def product_cost(parts, rows, feat):
    return pl.CostEstimate(
        flops=2 * parts * parts * rows * rows * feat,
        bytes_accessed=2 * parts * rows * (parts * rows + 2 * feat),
        transcendentals=0,
    )


def backward_kernel(dense_ref, *refs):
    parts = dense_ref.shape[0]
    sources, refs = refs[: parts * PIECES], refs[parts * PIECES :]
    keep_refs, pair_ref = refs[:2], refs[2]
    rows = sources[0].shape[0] * PIECES
    row, col = lax.axis_index("row"), lax.axis_index("col")
    for k in (1, 3, 0, 2):
        total = None
        for j in range(parts):
            where = pl.ds(pl.multiple_of((col ^ j) * rows, rows), rows)
            source = jnp.concatenate([sources[h * parts + j][...] for h in range(PIECES)], axis=0)
            term = lax.dot_general(
                dense_ref[row ^ k, where, :], source, (((0,), (0,)), ((), ())),
                preferred_element_type=F32,
            )
            total = term if total is None else total + term
        if k % 2:
            pair_ref[k // 2] = total.astype(BF)
        else:
            keep_refs[k // 2][...] = total


def backward(dense, sources):
    parts = len(sources) // PIECES
    rows, feat = sources[0].shape[0] * PIECES, sources[0].shape[1]
    return pl.pallas_call(
        backward_kernel,
        in_specs=[VMEM] * (1 + parts * PIECES),
        out_specs=[VMEM] * 3,
        out_shape=[
            jax.ShapeDtypeStruct((rows, feat), F32),
            jax.ShapeDtypeStruct((rows, feat), F32),
            jax.ShapeDtypeStruct((2, rows, feat), BF),
        ],
        compiler_params=pltpu.CompilerParams(vmem_limit_bytes=8 << 20),
        cost_estimate=product_cost(parts, rows, feat),
        name="backward",
    )(dense, *sources)


def pair_kernel(keep_ref, send_ref, arrived_ref, kept_ref, sent_ref):
    kept_ref[...] = keep_ref[...] + arrived_ref[0].astype(F32)
    sent_ref[...] = (send_ref[...] + arrived_ref[1].astype(F32)).astype(BF)


def pair_sum(keep, send, arrived):
    return pl.pallas_call(
        pair_kernel,
        in_specs=[VMEM] * 3,
        out_specs=[VMEM] * 2,
        out_shape=[
            jax.ShapeDtypeStruct(keep.shape, F32),
            jax.ShapeDtypeStruct(send.shape, BF),
        ],
        compiler_params=pltpu.CompilerParams(vmem_limit_bytes=8 << 20),
        cost_estimate=pl.CostEstimate(flops=3 * keep.size, bytes_accessed=20 * keep.size, transcendentals=0),
        name="pair_sum",
    )(keep, send, arrived)


def gradient_kernel(weight_ref, bias_ref, cot_ref, *refs):
    refs, (agg_ref, summed_ref, pre_ref, grad_ref) = refs[:-4], refs[-4:]
    terms = refs[:4]
    summed = terms[0][...].astype(F32)
    for term in terms[1:]:
        summed = summed + term[...].astype(F32)
    summed = summed.astype(BF)
    summed_ref[...] = summed
    pre = jnp.dot(summed, weight_ref[...], preferred_element_type=F32) + bias_ref[...]
    pre_ref[...] = pre
    sigma = jax.nn.sigmoid(pre)
    slope = sigma * (1.0 + pre * (1.0 - sigma))
    grad_pre = (cot_ref[...].astype(F32) * slope).astype(BF)
    grad_ref[...] = grad_pre
    agg_ref[...] = lax.dot_general(
        grad_pre, weight_ref[...], (((1,), (1,)), ((), ())), preferred_element_type=F32
    ).astype(BF)


def gradient(weight, bias, cot, terms, after, piece):
    rows, feat = terms[0].shape
    block = jax.ShapeDtypeStruct((rows, feat), BF)
    return pl.pallas_call(
        gradient_kernel,
        grid=(1,),
        in_specs=[VMEM, VMEM, pl.BlockSpec((rows, feat), lambda _: (piece, 0))]
        + [VMEM] * (len(terms) + len(after)),
        out_specs=[VMEM] * 4,
        out_shape=[block, block, jax.ShapeDtypeStruct((rows, feat), F32), block],
        compiler_params=pltpu.CompilerParams(vmem_limit_bytes=8 << 20),
        cost_estimate=pl.CostEstimate(
            flops=4 * rows * feat * feat, bytes_accessed=20 * rows * feat, transcendentals=rows * feat
        ),
        name="gradient",
    )(weight, bias, cot, *terms, *after)


def totals_kernel(after_ref, *refs):
    del after_ref
    summed_refs, pre_refs, grad_refs = (refs[i * PIECES : (i + 1) * PIECES] for i in range(3))
    hidden_ref, mine_ref, other_ref = refs[3 * PIECES :]
    height, feat = summed_refs[0].shape
    core = lax.axis_index("row") & 1
    for h in range(PIECES):
        pre = pre_refs[h][...]
        hidden_ref[h * height : (h + 1) * height, :] = (pre * jax.nn.sigmoid(pre)).astype(BF)
    grad_pre = jnp.concatenate([ref[...] for ref in grad_refs], axis=0)
    bias_row = jnp.sum(grad_pre.astype(F32), axis=0, keepdims=True)
    middle = feat // 2
    for target, index in ((mine_ref, core), (other_ref, 1 - core)):
        window = pl.ds(pl.multiple_of(index * middle, middle), middle)
        columns = jnp.concatenate([ref[:, window] for ref in summed_refs], axis=0)
        product = lax.dot_general(columns, grad_pre, (((0,), (0,)), ((), ())), preferred_element_type=F32)
        spread = jnp.broadcast_to(bias_row, (mine_ref.shape[0] - middle, feat))
        target[:middle, :] = product.astype(BF)
        target[middle:, :] = spread.astype(BF)


def totals(after, summed, pre, grad_pre):
    rows, feat = pre[0].shape[0] * PIECES, pre[0].shape[1]
    half = (feat // 2 + 16, feat)
    return pl.pallas_call(
        totals_kernel,
        in_specs=[VMEM] * (1 + 3 * PIECES),
        out_specs=[VMEM] * 3,
        out_shape=[
            jax.ShapeDtypeStruct((rows, feat), BF),
            jax.ShapeDtypeStruct(half, BF),
            jax.ShapeDtypeStruct(half, BF),
        ],
        compiler_params=pltpu.CompilerParams(vmem_limit_bytes=8 << 20),
        cost_estimate=pl.CostEstimate(
            flops=2 * rows * feat * feat, bytes_accessed=20 * rows * feat, transcendentals=rows * feat
        ),
        name="totals",
    )(after, *summed, *pre, *grad_pre)


def finish_kernel(scale, keep_ref, other_ref, half_ref, twin_ref, grad_ref, weight_ref, bias_ref):
    grad_ref[...] = (keep_ref[...] + other_ref[...].astype(F32)).astype(BF)
    part = weight_ref.shape[0] // 2
    core = lax.axis_index("row") & 1
    for k, share in enumerate((half_ref, twin_ref)):
        window = pl.ds(pl.multiple_of((core ^ k) * part, part), part)
        weight_ref[window, :] = share[:part, :] * scale
    bias_ref[...] = half_ref[part : part + 1, :] * scale


def finish(scale, keep, other, half, twin):
    feat = keep.shape[1]
    return pl.pallas_call(
        functools.partial(finish_kernel, scale),
        in_specs=[VMEM] * 4,
        out_specs=[VMEM] * 3,
        out_shape=[
            jax.ShapeDtypeStruct(keep.shape, BF),
            jax.ShapeDtypeStruct((feat, feat), F32),
            jax.ShapeDtypeStruct((1, feat), F32),
        ],
        compiler_params=pltpu.CompilerParams(vmem_limit_bytes=8 << 20),
        cost_estimate=pl.CostEstimate(flops=feat * feat, bytes_accessed=6 * feat * feat, transcendentals=0),
        name="finish",
    )(keep, other, half, twin)


def dense_device(features, weight, bias, tile_rows, tile_cols, tile_vals, tile_count, cotangent):
    own = features[0, 0]
    rows, feat = own.shape
    row = lax.axis_index("row")

    from_chip = swap(own, "row", 2)
    from_core = swap(own, "row", 1)
    dense = build_dense(tile_vals[0, 0], tile_rows[0, 0], tile_cols[0, 0], tile_count[0], 4, rows)
    dense, from_chip = lax.optimization_barrier((dense, from_chip))
    sources = [own, from_core, from_chip, swap(from_chip, "row", 1)]
    partial = forward(dense, sources)

    kept, gathered, after = [], [], []
    for h in range(PIECES):
        mine = partial[h * 4 : (h + 1) * 4]
        terms = [mine[0]] + [swap(mine[k], "col", k) for k in (3, 1, 2)]
        agg, *rest = gradient(weight, bias[None, :], cotangent[0, 0], terms, after, h)
        kept.append(rest)
        after = [agg]
        early = swap(agg, "col", 1)
        grads = {0: agg, 1: early}
        grads[2] = swap(agg, "col", 2)
        grads[1], grads[2] = lax.optimization_barrier((grads[1], grads[2]))
        grads[3] = swap(grads[2], "col", 1)
        gathered += [grads[k] for k in range(4)]

    hidden, mine, others = totals(agg, *zip(*kept))
    half = tree(mine, swap(others, "row", 1), swap(mine, "row", 2), swap(others, "row", 3)).astype(BF)

    keep, send, pair = backward(dense, gathered)
    keep, send = pair_sum(keep, send, swap(pair, "row", 1))

    half = tree(half, *(swap(half, "col", k) for k in (1, 2, 3)))
    twin = swap(half, "row", 1)
    grad_features, grad_weight, grad_bias = finish(
        float(rows * 16) ** (-0.5), keep, swap(send, "row", 2), half, twin
    )
    return (hidden[None, None], grad_features[None, None], grad_weight, grad_bias[0])


def per_device(features, weight, bias, tile_rows, tile_cols, tile_vals, tile_count, cotangent):
    rows = features.shape[2]
    slots, tile, _ = tile_vals.shape[2:]
    square = lax.axis_size("row") == 4 and lax.axis_size("col") == 4
    dense_fits = (4 * rows // tile) ** 2 <= slots
    chosen = dense_device if square and dense_fits else sparse_device
    return chosen(features, weight, bias, tile_rows, tile_cols, tile_vals, tile_count, cotangent)


def solution(mesh):
    placed = (
        P(("groups", "col"), "row", None, None),
        P(),
        P(),
        P(("groups", "row"), "col", None),
        P(("groups", "row"), "col", None),
        P(("groups", "row"), "col", None, None, None),
        P(("groups", "row"), "col"),
        P(("groups", "row"), "col", None, None),
    )
    return jax.shard_map(
        per_device,
        mesh=mesh,
        in_specs=placed,
        out_specs=(
            P(("groups", "row"), "col", None, None),
            P(("groups", "col"), "row", None, None),
            P("groups", None),
            P("groups"),
        ),
        check_vma=False,
    )
```

```python
import functools

import jax
import jax.numpy as jnp
from jax import lax
from jax.experimental import pallas as pl
from jax.experimental.pallas import tpu as pltpu
from jax.sharding import PartitionSpec as P

BF = jnp.bfloat16
F32 = jnp.float32
VMEM = pl.BlockSpec(memory_space=pltpu.VMEM)
HBM = pl.BlockSpec(memory_space=pltpu.HBM)
PIECES = 1


def tile_terms(values, picked, forward):
    if forward:
        return jnp.einsum("tij,tjf->tif", values, picked, preferred_element_type=jnp.float32)
    return jnp.einsum("tji,tjf->tif", values, picked, preferred_element_type=jnp.float32)


def every_slot(values, source_idx, target_idx, live_count, source, forward):
    width = min(16, values.shape[0])
    targets = source.shape[0]

    def advance(index, carry):
        start = index * width
        block_values = lax.dynamic_slice_in_dim(values, start, width, 0)
        block_source = lax.dynamic_slice_in_dim(source_idx, start, width, 0)
        block_target = lax.dynamic_slice_in_dim(target_idx, start, width, 0)
        picked = jnp.take(source, block_source, axis=0)
        terms = tile_terms(block_values, picked, forward)
        alive_mask = (start + jnp.arange(width) < live_count).astype(jnp.float32)
        placing = (jnp.arange(targets)[:, None] == block_target[None, :]).astype(jnp.float32)
        placing = placing * alive_mask[None, :]
        added = jnp.einsum("rt,tif->rif", placing, terms, precision=lax.Precision.HIGHEST)
        return carry + added

    initial = jnp.zeros(source.shape, jnp.float32)
    return lax.fori_loop(0, values.shape[0] // width, advance, initial)


def sparse_device(features, weight, bias, tile_rows, tile_cols, tile_vals, tile_count, cotangent):
    own_rows = features[0, 0]
    rows_dev, feat = own_rows.shape
    tile = tile_vals.shape[-1]
    values = tile_vals[0, 0]
    row_idx = tile_rows[0, 0]
    col_idx = tile_cols[0, 0]
    live_count = tile_count[0, 0]
    gathered = lax.all_gather(own_rows, "row", axis=0, tiled=True)
    block_nodes = gathered.shape[0]
    source = gathered.reshape(block_nodes // tile, tile, feat)
    forward_terms = every_slot(values, col_idx, row_idx, live_count, source, True)
    summed = lax.psum_scatter(
        forward_terms.reshape(block_nodes, feat).astype(BF), "col", scatter_dimension=0, tiled=True
    )
    pre = jnp.dot(summed, weight, preferred_element_type=F32) + bias
    hidden = jax.nn.silu(pre).astype(BF)
    sigma = jax.nn.sigmoid(pre)
    slope = sigma * (1.0 + pre * (1.0 - sigma))
    grad_pre = (cotangent[0, 0].astype(F32) * slope).astype(BF)
    weight_term = lax.dot_general(
        summed, grad_pre, (((0,), (0,)), ((), ())), preferred_element_type=F32
    )
    bias_term = jnp.sum(grad_pre.astype(F32), axis=0)
    weight_sum, bias_sum = lax.psum((weight_term, bias_term), ("row", "col"))
    node_total = rows_dev * lax.axis_size("row") * lax.axis_size("col")
    factor = float(node_total) ** (-0.5)
    grad_local = jnp.dot(grad_pre, weight.T, preferred_element_type=F32).astype(BF)
    grad_rows = lax.all_gather(grad_local, "col", axis=0, tiled=True)
    grad_source = grad_rows.reshape(block_nodes // tile, tile, feat)
    backward_terms = every_slot(values, row_idx, col_idx, live_count, grad_source, False)
    back_summed = lax.psum_scatter(
        backward_terms.reshape(block_nodes, feat).astype(BF), "row", scatter_dimension=0, tiled=True
    )
    hidden_out = hidden.reshape(1, 1, rows_dev, feat)
    grad_features = back_summed.reshape(1, 1, rows_dev, feat)
    return (hidden_out, grad_features, weight_sum * factor, bias_sum * factor)


def swap(x, axis, bit):
    size = lax.axis_size(axis)
    return lax.ppermute(x, axis, [(i, i ^ bit) for i in range(size)])


def tree(own, near, far, cross):
    own, near, far, cross = (x.astype(F32) for x in (own, near, far, cross))
    return (own + near) + (far + cross)


def build_kernel(slots_hbm, vals_hbm, dense_ref, slots_ref, vals_ref, total, sem):
    slots, tile, _ = vals_ref.shape
    chunks = sem.shape[0] - 1
    width = slots // chunks
    per = dense_ref.shape[2] // tile
    wide = total.shape[0]
    small = pltpu.make_async_copy(slots_hbm, slots_ref, sem.at[chunks])
    big = [
        pltpu.make_async_copy(
            vals_hbm.at[pl.ds(i * width, width)], vals_ref.at[pl.ds(i * width, width)], sem.at[i]
        )
        for i in range(chunks)
    ]
    small.start()
    for copy in big:
        copy.start()
    total[...] = jnp.zeros_like(total)
    small.wait()
    live = slots_ref[slots]

    def place(slot, carry):
        spot = slots_ref[slot]
        where = pl.ds(pl.multiple_of(lax.div(spot, wide) * tile, tile), tile)
        total[lax.rem(spot, wide), where, :] += vals_ref[slot].astype(F32)
        return carry

    for i in range(chunks):
        big[i].wait()
        lax.fori_loop(i * width, jnp.clip(live, i * width, (i + 1) * width), place, 0)

    for col in range(wide):
        dense_ref[col // per, :, (col % per) * tile : (col % per + 1) * tile] = total[col].astype(BF)


def build_dense(values, row_idx, col_idx, count, parts, rows_dev):
    slots, tile, _ = values.shape
    nodes = parts * rows_dev
    wide = nodes // tile
    chunks = 8
    listed = jnp.concatenate([row_idx * wide + col_idx, jnp.broadcast_to(count, (slots,))])
    return pl.pallas_call(
        build_kernel,
        in_specs=[HBM] * 2,
        out_specs=VMEM,
        out_shape=jax.ShapeDtypeStruct((parts, nodes, rows_dev), BF),
        scratch_shapes=[
            pltpu.SMEM(listed.shape, jnp.int32),
            pltpu.VMEM(values.shape, BF),
            pltpu.VMEM((wide, nodes, tile), F32),
            pltpu.SemaphoreType.DMA((chunks + 1,)),
        ],
        compiler_params=pltpu.CompilerParams(vmem_limit_bytes=50 << 20),
        cost_estimate=pl.CostEstimate(flops=8 * nodes * nodes, bytes_accessed=6 * nodes * nodes, transcendentals=0),
        name="build_dense",
    )(listed, values)


def forward_kernel(dense_ref, *refs):
    parts = dense_ref.shape[0]
    sources, outs = refs[:parts], refs[parts:]
    rows = sources[0].shape[0]
    row, col = lax.axis_index("row"), lax.axis_index("col")
    for k in range(parts):
        where = pl.ds(pl.multiple_of((col ^ k) * rows, rows), rows)
        total = None
        for j in range(parts):
            term = jnp.dot(dense_ref[row ^ j, where, :], sources[j][...], preferred_element_type=F32)
            total = term if total is None else total + term
        total = total.astype(BF)
        for h in range(PIECES):
            height = rows // PIECES
            outs[h * parts + k][...] = total[h * height : (h + 1) * height]


def forward(dense, sources):
    parts = len(sources)
    rows, feat = sources[0].shape
    return pl.pallas_call(
        forward_kernel,
        in_specs=[VMEM] * (1 + parts),
        out_specs=[VMEM] * (parts * PIECES),
        out_shape=[jax.ShapeDtypeStruct((rows // PIECES, feat), BF)] * (parts * PIECES),
        compiler_params=pltpu.CompilerParams(vmem_limit_bytes=8 << 20),
        cost_estimate=product_cost(parts, rows, feat),
        name="forward",
    )(dense, *sources)


def product_cost(parts, rows, feat):
    return pl.CostEstimate(
        flops=2 * parts * parts * rows * rows * feat,
        bytes_accessed=2 * parts * rows * (parts * rows + 2 * feat),
        transcendentals=0,
    )


def backward_kernel(dense_ref, *refs):
    parts = dense_ref.shape[0]
    sources, refs = refs[: parts * PIECES], refs[parts * PIECES :]
    keep_refs, pair_ref = refs[:2], refs[2]
    rows = sources[0].shape[0] * PIECES
    row, col = lax.axis_index("row"), lax.axis_index("col")
    for k in (1, 3, 0, 2):
        total = None
        for j in range(parts):
            where = pl.ds(pl.multiple_of((col ^ j) * rows, rows), rows)
            source = jnp.concatenate([sources[h * parts + j][...] for h in range(PIECES)], axis=0)
            term = lax.dot_general(
                dense_ref[row ^ k, where, :], source, (((0,), (0,)), ((), ())),
                preferred_element_type=F32,
            )
            total = term if total is None else total + term
        if k % 2:
            pair_ref[k // 2] = total.astype(BF)
        else:
            keep_refs[k // 2][...] = total


def backward(dense, sources):
    parts = len(sources) // PIECES
    rows, feat = sources[0].shape[0] * PIECES, sources[0].shape[1]
    return pl.pallas_call(
        backward_kernel,
        in_specs=[VMEM] * (1 + parts * PIECES),
        out_specs=[VMEM] * 3,
        out_shape=[
            jax.ShapeDtypeStruct((rows, feat), F32),
            jax.ShapeDtypeStruct((rows, feat), F32),
            jax.ShapeDtypeStruct((2, rows, feat), BF),
        ],
        compiler_params=pltpu.CompilerParams(vmem_limit_bytes=8 << 20),
        cost_estimate=product_cost(parts, rows, feat),
        name="backward",
    )(dense, *sources)


def pair_kernel(keep_ref, send_ref, arrived_ref, kept_ref, sent_ref):
    kept_ref[...] = keep_ref[...] + arrived_ref[0].astype(F32)
    sent_ref[...] = (send_ref[...] + arrived_ref[1].astype(F32)).astype(BF)


def pair_sum(keep, send, arrived):
    return pl.pallas_call(
        pair_kernel,
        in_specs=[VMEM] * 3,
        out_specs=[VMEM] * 2,
        out_shape=[
            jax.ShapeDtypeStruct(keep.shape, F32),
            jax.ShapeDtypeStruct(send.shape, BF),
        ],
        compiler_params=pltpu.CompilerParams(vmem_limit_bytes=8 << 20),
        cost_estimate=pl.CostEstimate(flops=3 * keep.size, bytes_accessed=20 * keep.size, transcendentals=0),
        name="pair_sum",
    )(keep, send, arrived)


def gradient_kernel(weight_ref, bias_ref, cot_ref, *refs):
    refs, (agg_ref, summed_ref, pre_ref, grad_ref) = refs[:-4], refs[-4:]
    terms = refs[:4]
    summed = terms[0][...].astype(F32)
    for term in terms[1:]:
        summed = summed + term[...].astype(F32)
    summed = summed.astype(BF)
    summed_ref[...] = summed
    pre = jnp.dot(summed, weight_ref[...], preferred_element_type=F32) + bias_ref[...]
    pre_ref[...] = pre
    sigma = jax.nn.sigmoid(pre)
    slope = sigma * (1.0 + pre * (1.0 - sigma))
    grad_pre = (cot_ref[...].astype(F32) * slope).astype(BF)
    grad_ref[...] = grad_pre
    agg_ref[...] = lax.dot_general(
        grad_pre, weight_ref[...], (((1,), (1,)), ((), ())), preferred_element_type=F32
    ).astype(BF)


def gradient(weight, bias, cot, terms, after, piece):
    rows, feat = terms[0].shape
    block = jax.ShapeDtypeStruct((rows, feat), BF)
    return pl.pallas_call(
        gradient_kernel,
        grid=(1,),
        in_specs=[VMEM, VMEM, pl.BlockSpec((rows, feat), lambda _: (piece, 0))]
        + [VMEM] * (len(terms) + len(after)),
        out_specs=[VMEM] * 4,
        out_shape=[block, block, jax.ShapeDtypeStruct((rows, feat), F32), block],
        compiler_params=pltpu.CompilerParams(vmem_limit_bytes=8 << 20),
        cost_estimate=pl.CostEstimate(
            flops=4 * rows * feat * feat, bytes_accessed=20 * rows * feat, transcendentals=rows * feat
        ),
        name="gradient",
    )(weight, bias, cot, *terms, *after)


def totals_kernel(after_ref, *refs):
    del after_ref
    summed_refs, grad_refs = refs[:PIECES], refs[PIECES : 2 * PIECES]
    mine_ref, other_ref = refs[2 * PIECES :]
    feat = summed_refs[0].shape[1]
    core = lax.axis_index("row") & 1
    grad_pre = jnp.concatenate([ref[...] for ref in grad_refs], axis=0)
    bias_row = jnp.sum(grad_pre.astype(F32), axis=0, keepdims=True)
    middle = feat // 2
    for target, index in ((mine_ref, core), (other_ref, 1 - core)):
        window = pl.ds(pl.multiple_of(index * middle, middle), middle)
        columns = jnp.concatenate([ref[:, window] for ref in summed_refs], axis=0)
        product = lax.dot_general(columns, grad_pre, (((0,), (0,)), ((), ())), preferred_element_type=F32)
        spread = jnp.broadcast_to(bias_row, (mine_ref.shape[0] - middle, feat))
        target[:middle, :] = product.astype(BF)
        target[middle:, :] = spread.astype(BF)


def totals(after, summed, grad_pre):
    rows, feat = summed[0].shape[0] * PIECES, summed[0].shape[1]
    half = (feat // 2 + 16, feat)
    return pl.pallas_call(
        totals_kernel,
        in_specs=[VMEM] * (1 + 2 * PIECES),
        out_specs=[VMEM] * 2,
        out_shape=[
            jax.ShapeDtypeStruct(half, BF),
            jax.ShapeDtypeStruct(half, BF),
        ],
        compiler_params=pltpu.CompilerParams(vmem_limit_bytes=8 << 20),
        cost_estimate=pl.CostEstimate(
            flops=2 * rows * feat * feat, bytes_accessed=20 * rows * feat, transcendentals=rows * feat
        ),
        name="totals",
    )(after, *summed, *grad_pre)


def finish_kernel(scale, keep_ref, other_ref, half_ref, twin_ref, grad_ref, weight_ref, bias_ref):
    grad_ref[...] = (keep_ref[...] + other_ref[...].astype(F32)).astype(BF)
    part = weight_ref.shape[0] // 2
    core = lax.axis_index("row") & 1
    for k, share in enumerate((half_ref, twin_ref)):
        window = pl.ds(pl.multiple_of((core ^ k) * part, part), part)
        weight_ref[window, :] = share[:part, :] * scale
    bias_ref[...] = half_ref[part : part + 1, :] * scale


def finish(scale, keep, other, half, twin):
    feat = keep.shape[1]
    return pl.pallas_call(
        functools.partial(finish_kernel, scale),
        in_specs=[VMEM] * 4,
        out_specs=[VMEM] * 3,
        out_shape=[
            jax.ShapeDtypeStruct(keep.shape, BF),
            jax.ShapeDtypeStruct((feat, feat), F32),
            jax.ShapeDtypeStruct((1, feat), F32),
        ],
        compiler_params=pltpu.CompilerParams(vmem_limit_bytes=8 << 20),
        cost_estimate=pl.CostEstimate(flops=feat * feat, bytes_accessed=6 * feat * feat, transcendentals=0),
        name="finish",
    )(keep, other, half, twin)


def dense_device(features, weight, bias, tile_rows, tile_cols, tile_vals, tile_count, cotangent):
    own = features[0, 0]
    rows, feat = own.shape
    row = lax.axis_index("row")

    from_chip = swap(own, "row", 2)
    from_core = swap(own, "row", 1)
    dense = build_dense(tile_vals[0, 0], tile_rows[0, 0], tile_cols[0, 0], tile_count[0], 4, rows)
    dense, from_chip = lax.optimization_barrier((dense, from_chip))
    sources = [own, from_core, from_chip, swap(from_chip, "row", 1)]
    partial = forward(dense, sources)

    kept, gathered, after = [], [], []
    for h in range(PIECES):
        mine = partial[h * 4 : (h + 1) * 4]
        terms = [mine[0]] + [swap(mine[k], "col", k) for k in (3, 1, 2)]
        agg, *rest = gradient(weight, bias[None, :], cotangent[0, 0], terms, after, h)
        kept.append(rest)
        after = [agg]
        early = swap(agg, "col", 1)
        grads = {0: agg, 1: early}
        grads[2] = swap(agg, "col", 2)
        grads[1], grads[2] = lax.optimization_barrier((grads[1], grads[2]))
        grads[3] = swap(grads[2], "col", 1)
        gathered += [grads[k] for k in range(4)]

    summed, pre, grad_pre = zip(*kept)
    mine, others = totals(agg, summed, grad_pre)
    hidden = jax.nn.silu(jnp.concatenate(pre, axis=0)).astype(BF)
    half = tree(mine, swap(others, "row", 1), swap(mine, "row", 2), swap(others, "row", 3)).astype(BF)

    keep, send, pair = backward(dense, gathered)
    keep, send = pair_sum(keep, send, swap(pair, "row", 1))

    half = tree(half, *(swap(half, "col", k) for k in (1, 2, 3)))
    half, keep = lax.optimization_barrier((half, keep))
    twin = swap(half, "row", 1)
    grad_features, grad_weight, grad_bias = finish(
        float(rows * 16) ** (-0.5), keep, swap(send, "row", 2), half, twin
    )
    return (hidden[None, None], grad_features[None, None], grad_weight, grad_bias[0])


def per_device(features, weight, bias, tile_rows, tile_cols, tile_vals, tile_count, cotangent):
    rows = features.shape[2]
    slots, tile, _ = tile_vals.shape[2:]
    square = lax.axis_size("row") == 4 and lax.axis_size("col") == 4
    dense_fits = (4 * rows // tile) ** 2 <= slots
    chosen = dense_device if square and dense_fits else sparse_device
    return chosen(features, weight, bias, tile_rows, tile_cols, tile_vals, tile_count, cotangent)


def solution(mesh):
    placed = (
        P(("groups", "col"), "row", None, None),
        P(),
        P(),
        P(("groups", "row"), "col", None),
        P(("groups", "row"), "col", None),
        P(("groups", "row"), "col", None, None, None),
        P(("groups", "row"), "col"),
        P(("groups", "row"), "col", None, None),
    )
    return jax.shard_map(
        per_device,
        mesh=mesh,
        in_specs=placed,
        out_specs=(
            P(("groups", "row"), "col", None, None),
            P(("groups", "col"), "row", None, None),
            P("groups", None),
            P("groups"),
        ),
        check_vma=False,
    )
```

```python
import functools

import jax
import jax.numpy as jnp
from jax import lax
from jax.experimental import pallas as pl
from jax.experimental.pallas import tpu as pltpu
from jax.sharding import PartitionSpec as P

BF = jnp.bfloat16
F32 = jnp.float32
VMEM = pl.BlockSpec(memory_space=pltpu.VMEM)
HBM = pl.BlockSpec(memory_space=pltpu.HBM)
PIECES = 1


def tile_terms(values, picked, forward):
    if forward:
        return jnp.einsum("tij,tjf->tif", values, picked, preferred_element_type=jnp.float32)
    return jnp.einsum("tji,tjf->tif", values, picked, preferred_element_type=jnp.float32)


def every_slot(values, source_idx, target_idx, live_count, source, forward):
    width = min(16, values.shape[0])
    targets = source.shape[0]

    def advance(index, carry):
        start = index * width
        block_values = lax.dynamic_slice_in_dim(values, start, width, 0)
        block_source = lax.dynamic_slice_in_dim(source_idx, start, width, 0)
        block_target = lax.dynamic_slice_in_dim(target_idx, start, width, 0)
        picked = jnp.take(source, block_source, axis=0)
        terms = tile_terms(block_values, picked, forward)
        alive_mask = (start + jnp.arange(width) < live_count).astype(jnp.float32)
        placing = (jnp.arange(targets)[:, None] == block_target[None, :]).astype(jnp.float32)
        placing = placing * alive_mask[None, :]
        added = jnp.einsum("rt,tif->rif", placing, terms, precision=lax.Precision.HIGHEST)
        return carry + added

    initial = jnp.zeros(source.shape, jnp.float32)
    return lax.fori_loop(0, values.shape[0] // width, advance, initial)


def sparse_device(features, weight, bias, tile_rows, tile_cols, tile_vals, tile_count, cotangent):
    own_rows = features[0, 0]
    rows_dev, feat = own_rows.shape
    tile = tile_vals.shape[-1]
    values = tile_vals[0, 0]
    row_idx = tile_rows[0, 0]
    col_idx = tile_cols[0, 0]
    live_count = tile_count[0, 0]
    gathered = lax.all_gather(own_rows, "row", axis=0, tiled=True)
    block_nodes = gathered.shape[0]
    source = gathered.reshape(block_nodes // tile, tile, feat)
    forward_terms = every_slot(values, col_idx, row_idx, live_count, source, True)
    summed = lax.psum_scatter(
        forward_terms.reshape(block_nodes, feat).astype(BF), "col", scatter_dimension=0, tiled=True
    )
    pre = jnp.dot(summed, weight, preferred_element_type=F32) + bias
    hidden = jax.nn.silu(pre).astype(BF)
    sigma = jax.nn.sigmoid(pre)
    slope = sigma * (1.0 + pre * (1.0 - sigma))
    grad_pre = (cotangent[0, 0].astype(F32) * slope).astype(BF)
    weight_term = lax.dot_general(
        summed, grad_pre, (((0,), (0,)), ((), ())), preferred_element_type=F32
    )
    bias_term = jnp.sum(grad_pre.astype(F32), axis=0)
    weight_sum, bias_sum = lax.psum((weight_term, bias_term), ("row", "col"))
    node_total = rows_dev * lax.axis_size("row") * lax.axis_size("col")
    factor = float(node_total) ** (-0.5)
    grad_local = jnp.dot(grad_pre, weight.T, preferred_element_type=F32).astype(BF)
    grad_rows = lax.all_gather(grad_local, "col", axis=0, tiled=True)
    grad_source = grad_rows.reshape(block_nodes // tile, tile, feat)
    backward_terms = every_slot(values, row_idx, col_idx, live_count, grad_source, False)
    back_summed = lax.psum_scatter(
        backward_terms.reshape(block_nodes, feat).astype(BF), "row", scatter_dimension=0, tiled=True
    )
    hidden_out = hidden.reshape(1, 1, rows_dev, feat)
    grad_features = back_summed.reshape(1, 1, rows_dev, feat)
    return (hidden_out, grad_features, weight_sum * factor, bias_sum * factor)


def swap(x, axis, bit):
    size = lax.axis_size(axis)
    return lax.ppermute(x, axis, [(i, i ^ bit) for i in range(size)])


def tree(own, near, far, cross):
    own, near, far, cross = (x.astype(F32) for x in (own, near, far, cross))
    return (own + near) + (far + cross)


def build_kernel(slots_hbm, vals_hbm, dense_ref, slots_ref, vals_ref, total, sem):
    slots, tile, _ = vals_ref.shape
    chunks = sem.shape[0] - 1
    width = slots // chunks
    per = dense_ref.shape[2] // tile
    wide = total.shape[0]
    small = pltpu.make_async_copy(slots_hbm, slots_ref, sem.at[chunks])
    big = [
        pltpu.make_async_copy(
            vals_hbm.at[pl.ds(i * width, width)], vals_ref.at[pl.ds(i * width, width)], sem.at[i]
        )
        for i in range(chunks)
    ]
    small.start()
    for copy in big:
        copy.start()
    total[...] = jnp.zeros_like(total)
    small.wait()
    live = slots_ref[slots]

    def place(slot, carry):
        spot = slots_ref[slot]
        where = pl.ds(pl.multiple_of(lax.div(spot, wide) * tile, tile), tile)
        total[lax.rem(spot, wide), where, :] += vals_ref[slot].astype(F32)
        return carry

    for i in range(chunks):
        big[i].wait()
        lax.fori_loop(i * width, jnp.clip(live, i * width, (i + 1) * width), place, 0)

    for col in range(wide):
        dense_ref[col // per, :, (col % per) * tile : (col % per + 1) * tile] = total[col].astype(BF)


def build_dense(values, row_idx, col_idx, count, parts, rows_dev):
    slots, tile, _ = values.shape
    nodes = parts * rows_dev
    wide = nodes // tile
    chunks = 8
    listed = jnp.concatenate([row_idx * wide + col_idx, jnp.broadcast_to(count, (slots,))])
    return pl.pallas_call(
        build_kernel,
        in_specs=[HBM] * 2,
        out_specs=VMEM,
        out_shape=jax.ShapeDtypeStruct((parts, nodes, rows_dev), BF),
        scratch_shapes=[
            pltpu.SMEM(listed.shape, jnp.int32),
            pltpu.VMEM(values.shape, BF),
            pltpu.VMEM((wide, nodes, tile), F32),
            pltpu.SemaphoreType.DMA((chunks + 1,)),
        ],
        compiler_params=pltpu.CompilerParams(vmem_limit_bytes=50 << 20),
        cost_estimate=pl.CostEstimate(flops=8 * nodes * nodes, bytes_accessed=6 * nodes * nodes, transcendentals=0),
        name="build_dense",
    )(listed, values)


def forward_kernel(dense_ref, *refs):
    parts = dense_ref.shape[0]
    sources, outs = refs[:parts], refs[parts:]
    rows = sources[0].shape[0]
    row, col = lax.axis_index("row"), lax.axis_index("col")
    for k in range(parts):
        where = pl.ds(pl.multiple_of((col ^ k) * rows, rows), rows)
        total = None
        for j in range(parts):
            term = jnp.dot(dense_ref[row ^ j, where, :], sources[j][...], preferred_element_type=F32)
            total = term if total is None else total + term
        total = total.astype(BF)
        for h in range(PIECES):
            height = rows // PIECES
            outs[h * parts + k][...] = total[h * height : (h + 1) * height]


def forward(dense, sources):
    parts = len(sources)
    rows, feat = sources[0].shape
    return pl.pallas_call(
        forward_kernel,
        in_specs=[VMEM] * (1 + parts),
        out_specs=[VMEM] * (parts * PIECES),
        out_shape=[jax.ShapeDtypeStruct((rows // PIECES, feat), BF)] * (parts * PIECES),
        compiler_params=pltpu.CompilerParams(vmem_limit_bytes=8 << 20),
        cost_estimate=product_cost(parts, rows, feat),
        name="forward",
    )(dense, *sources)


def product_cost(parts, rows, feat):
    return pl.CostEstimate(
        flops=2 * parts * parts * rows * rows * feat,
        bytes_accessed=2 * parts * rows * (parts * rows + 2 * feat),
        transcendentals=0,
    )


def backward_kernel(dense_ref, *refs):
    parts = dense_ref.shape[0]
    sources, refs = refs[: parts * PIECES], refs[parts * PIECES :]
    keep_refs, pair_ref = refs[:2], refs[2]
    rows = sources[0].shape[0] * PIECES
    row, col = lax.axis_index("row"), lax.axis_index("col")
    for k in (1, 3, 0, 2):
        total = None
        for j in range(parts):
            where = pl.ds(pl.multiple_of((col ^ j) * rows, rows), rows)
            source = jnp.concatenate([sources[h * parts + j][...] for h in range(PIECES)], axis=0)
            term = lax.dot_general(
                dense_ref[row ^ k, where, :], source, (((0,), (0,)), ((), ())),
                preferred_element_type=F32,
            )
            total = term if total is None else total + term
        if k % 2:
            pair_ref[k // 2] = total.astype(BF)
        else:
            keep_refs[k // 2][...] = total


def backward(dense, sources):
    parts = len(sources) // PIECES
    rows, feat = sources[0].shape[0] * PIECES, sources[0].shape[1]
    return pl.pallas_call(
        backward_kernel,
        in_specs=[VMEM] * (1 + parts * PIECES),
        out_specs=[VMEM] * 3,
        out_shape=[
            jax.ShapeDtypeStruct((rows, feat), F32),
            jax.ShapeDtypeStruct((rows, feat), F32),
            jax.ShapeDtypeStruct((2, rows, feat), BF),
        ],
        compiler_params=pltpu.CompilerParams(vmem_limit_bytes=8 << 20),
        cost_estimate=product_cost(parts, rows, feat),
        name="backward",
    )(dense, *sources)


def pair_kernel(keep_ref, send_ref, arrived_ref, kept_ref, sent_ref):
    kept_ref[...] = keep_ref[...] + arrived_ref[0].astype(F32)
    sent_ref[...] = (send_ref[...] + arrived_ref[1].astype(F32)).astype(BF)


def pair_sum(keep, send, arrived):
    return pl.pallas_call(
        pair_kernel,
        in_specs=[VMEM] * 3,
        out_specs=[VMEM] * 2,
        out_shape=[
            jax.ShapeDtypeStruct(keep.shape, F32),
            jax.ShapeDtypeStruct(send.shape, BF),
        ],
        compiler_params=pltpu.CompilerParams(vmem_limit_bytes=8 << 20),
        cost_estimate=pl.CostEstimate(flops=3 * keep.size, bytes_accessed=20 * keep.size, transcendentals=0),
        name="pair_sum",
    )(keep, send, arrived)


def gradient_kernel(weight_ref, bias_ref, cot_ref, *refs):
    refs, (agg_ref, summed_ref, pre_ref, grad_ref) = refs[:-4], refs[-4:]
    terms = refs[:4]
    summed = terms[0][...].astype(F32)
    for term in terms[1:]:
        summed = summed + term[...].astype(F32)
    summed = summed.astype(BF)
    summed_ref[...] = summed
    pre = jnp.dot(summed, weight_ref[...], preferred_element_type=F32) + bias_ref[...]
    pre_ref[...] = pre
    sigma = jax.nn.sigmoid(pre)
    slope = sigma * (1.0 + pre * (1.0 - sigma))
    grad_pre = (cot_ref[...].astype(F32) * slope).astype(BF)
    grad_ref[...] = grad_pre
    agg_ref[...] = lax.dot_general(
        grad_pre, weight_ref[...], (((1,), (1,)), ((), ())), preferred_element_type=F32
    ).astype(BF)


def gradient(weight, bias, cot, terms, after, piece):
    rows, feat = terms[0].shape
    block = jax.ShapeDtypeStruct((rows, feat), BF)
    return pl.pallas_call(
        gradient_kernel,
        grid=(1,),
        in_specs=[VMEM, VMEM, pl.BlockSpec((rows, feat), lambda _: (piece, 0))]
        + [VMEM] * (len(terms) + len(after)),
        out_specs=[VMEM] * 4,
        out_shape=[block, block, jax.ShapeDtypeStruct((rows, feat), F32), block],
        compiler_params=pltpu.CompilerParams(vmem_limit_bytes=8 << 20),
        cost_estimate=pl.CostEstimate(
            flops=4 * rows * feat * feat, bytes_accessed=20 * rows * feat, transcendentals=rows * feat
        ),
        name="gradient",
    )(weight, bias, cot, *terms, *after)


def totals_kernel(after_ref, *refs):
    del after_ref
    summed_refs, grad_refs = refs[:PIECES], refs[PIECES : 2 * PIECES]
    mine_ref, other_ref = refs[2 * PIECES :]
    feat = summed_refs[0].shape[1]
    core = lax.axis_index("row") & 1
    grad_pre = jnp.concatenate([ref[...] for ref in grad_refs], axis=0)
    bias_row = jnp.sum(grad_pre.astype(F32), axis=0, keepdims=True)
    middle = feat // 2
    for target, index in ((mine_ref, core), (other_ref, 1 - core)):
        window = pl.ds(pl.multiple_of(index * middle, middle), middle)
        columns = jnp.concatenate([ref[:, window] for ref in summed_refs], axis=0)
        product = lax.dot_general(columns, grad_pre, (((0,), (0,)), ((), ())), preferred_element_type=F32)
        spread = jnp.broadcast_to(bias_row, (mine_ref.shape[0] - middle, feat))
        target[:middle, :] = product.astype(BF)
        target[middle:, :] = spread.astype(BF)


def totals(after, summed, grad_pre):
    rows, feat = summed[0].shape[0] * PIECES, summed[0].shape[1]
    half = (feat // 2 + 16, feat)
    return pl.pallas_call(
        totals_kernel,
        in_specs=[VMEM] * (1 + 2 * PIECES),
        out_specs=[VMEM] * 2,
        out_shape=[
            jax.ShapeDtypeStruct(half, BF),
            jax.ShapeDtypeStruct(half, BF),
        ],
        compiler_params=pltpu.CompilerParams(vmem_limit_bytes=8 << 20),
        cost_estimate=pl.CostEstimate(
            flops=2 * rows * feat * feat, bytes_accessed=20 * rows * feat, transcendentals=rows * feat
        ),
        name="totals",
    )(after, *summed, *grad_pre)


def finish_kernel(scale, keep_ref, other_ref, half_ref, twin_ref, grad_ref, weight_ref, bias_ref):
    grad_ref[...] = (keep_ref[...] + other_ref[...].astype(F32)).astype(BF)
    part = weight_ref.shape[0] // 2
    core = lax.axis_index("row") & 1
    for k, share in enumerate((half_ref, twin_ref)):
        window = pl.ds(pl.multiple_of((core ^ k) * part, part), part)
        weight_ref[window, :] = share[:part, :] * scale
    bias_ref[...] = half_ref[part : part + 1, :] * scale


def finish(scale, keep, other, half, twin):
    feat = keep.shape[1]
    return pl.pallas_call(
        functools.partial(finish_kernel, scale),
        in_specs=[VMEM] * 4,
        out_specs=[VMEM] * 3,
        out_shape=[
            jax.ShapeDtypeStruct(keep.shape, BF),
            jax.ShapeDtypeStruct((feat, feat), F32),
            jax.ShapeDtypeStruct((1, feat), F32),
        ],
        compiler_params=pltpu.CompilerParams(vmem_limit_bytes=8 << 20),
        cost_estimate=pl.CostEstimate(flops=feat * feat, bytes_accessed=6 * feat * feat, transcendentals=0),
        name="finish",
    )(keep, other, half, twin)


def dense_device(features, weight, bias, tile_rows, tile_cols, tile_vals, tile_count, cotangent):
    own = features[0, 0]
    rows, feat = own.shape
    row = lax.axis_index("row")

    from_chip = swap(own, "row", 2)
    from_core = swap(own, "row", 1)
    dense = build_dense(tile_vals[0, 0], tile_rows[0, 0], tile_cols[0, 0], tile_count[0], 4, rows)
    dense, from_chip = lax.optimization_barrier((dense, from_chip))
    sources = [own, from_core, from_chip, swap(from_chip, "row", 1)]
    partial = forward(dense, sources)

    kept, gathered, after = [], [], []
    for h in range(PIECES):
        mine = partial[h * 4 : (h + 1) * 4]
        terms = [mine[0]] + [swap(mine[k], "col", k) for k in (3, 2, 1)]
        agg, *rest = gradient(weight, bias[None, :], cotangent[0, 0], terms, after, h)
        kept.append(rest)
        after = [agg]
        early = swap(agg, "col", 1)
        grads = {0: agg, 1: early}
        grads[2] = swap(agg, "col", 2)
        grads[1], grads[2] = lax.optimization_barrier((grads[1], grads[2]))
        grads[3] = swap(grads[2], "col", 1)
        gathered += [grads[k] for k in range(4)]

    summed, pre, grad_pre = zip(*kept)
    mine, others = totals(agg, summed, grad_pre)
    hidden = jax.nn.silu(jnp.concatenate(pre, axis=0)).astype(BF)
    half = tree(mine, swap(others, "row", 1), swap(mine, "row", 2), swap(others, "row", 3)).astype(BF)

    keep, send, pair = backward(dense, gathered)
    keep, send = pair_sum(keep, send, swap(pair, "row", 1))

    half = tree(half, *(swap(half, "col", k) for k in (1, 2, 3)))
    half, keep = lax.optimization_barrier((half, keep))
    twin = swap(half, "row", 1)
    grad_features, grad_weight, grad_bias = finish(
        float(rows * 16) ** (-0.5), keep, swap(send, "row", 2), half, twin
    )
    return (hidden[None, None], grad_features[None, None], grad_weight, grad_bias[0])


def per_device(features, weight, bias, tile_rows, tile_cols, tile_vals, tile_count, cotangent):
    rows = features.shape[2]
    slots, tile, _ = tile_vals.shape[2:]
    square = lax.axis_size("row") == 4 and lax.axis_size("col") == 4
    dense_fits = (4 * rows // tile) ** 2 <= slots
    chosen = dense_device if square and dense_fits else sparse_device
    return chosen(features, weight, bias, tile_rows, tile_cols, tile_vals, tile_count, cotangent)


def solution(mesh):
    placed = (
        P(("groups", "col"), "row", None, None),
        P(),
        P(),
        P(("groups", "row"), "col", None),
        P(("groups", "row"), "col", None),
        P(("groups", "row"), "col", None, None, None),
        P(("groups", "row"), "col"),
        P(("groups", "row"), "col", None, None),
    )
    return jax.shard_map(
        per_device,
        mesh=mesh,
        in_specs=placed,
        out_specs=(
            P(("groups", "row"), "col", None, None),
            P(("groups", "col"), "row", None, None),
            P("groups", None),
            P("groups"),
        ),
        check_vma=False,
    )
```
